128 devices in a mesh: row: 32 (over z, x, core), rep: 4 (over y).
Axes of the slice: x: 4, y: 4, z: 4, core: 2. Of those that a mesh axis runs over, the one named last changes fastest.
Arguments:
- grad_out: bfloat16 [65536, 256], P(('row', 'rep')), may hold values from -6 to 6
- preact: bfloat16 [65536, 256], P(('row', 'rep')), may hold values from -6 to 6
- features: bfloat16 [65536, 256], P(('row', 'rep')), may hold values from -6 to 6
- weight: bfloat16 [256, 256], replicated, may hold values from -0.375 to 0.375
- adj_values: bfloat16 [512, 128, 128, 128], P('row', 'rep'), may hold values from -0.0625 to 0.0625
- adj_cols: int32 [512, 128], P('row', 'rep'), may hold values from 0 to 511, as said below
- adj_counts: int32 [512, 4], P('row', 'rep'), may hold values from 1 to 32, as said below
Outputs:
- grad_features: bfloat16 [65536, 256], P(('row', 'rep'))
- grad_weight: float32 [256, 256], replicated
The draws below stay inside these ranges and needn't reach their ends.
Inputs may be any that keep to these rules, and one draw needn't show every extreme that they name: `adj_cols`: the stored block at slot p * 32 + s of a block row has a column block j with (j % 16) // 4 == p; the column blocks of one block row are all different; blocks past the live count still carry a valid column block. `adj_counts`: some entry equals 32.
All inputs are finite; a program needn't handle non-finite values.
Results may differ from the reference program's by a relative error of at most 0.019.
Values may be sent and summed in bfloat16 or wider, within the bound.
No kernel may reach another device: no remote copies, remote signals or barrier semaphores. Data moves between devices by JAX's collectives and lax.ppermute only.
A program may use at most 128 MiB of HBM per device.

```python
import jax
import jax.numpy as jnp
from jax import lax

F = 256
BLOCK = 128
ROWBLK = 16
SLOTS = 32
SHARE_BLOCKS = 4
NBR = 512
NODES = 65536
N_ROW = 32
N_REP = 4


def draw_adj_cols(key, part):
    key = jax.random.fold_in(key, 11)
    candidates = N_ROW * SHARE_BLOCKS
    keys = jax.random.split(key, NBR * N_REP)
    orders = jax.vmap(lambda k: jax.random.permutation(k, candidates))(keys)
    picked = orders[:, :SLOTS].astype(jnp.int32).reshape(NBR, N_REP, SLOTS)
    target_group = picked // SHARE_BLOCKS
    within = picked % SHARE_BLOCKS
    share_ids = jnp.arange(N_REP, dtype=jnp.int32)[None, :, None]
    columns = target_group * ROWBLK + share_ids * SHARE_BLOCKS + within
    return columns.reshape(NBR, N_REP * SLOTS).astype(jnp.int32)


def draw_adj_counts(key, part):
    key = jax.random.fold_in(key, 23)
    first, second = jax.random.split(key)
    counts = jax.random.randint(first, (NBR * N_REP,), 1, SLOTS + 1)
    chosen = jax.random.randint(second, (), 0, NBR * N_REP)
    counts = counts.at[chosen].set(SLOTS)
    return counts.reshape(NBR, N_REP).astype(jnp.int32)


def shard_levels(stream_key, extent, cuts, smallest, high):
    gain = 1.0
    for axis_at, shards_of in cuts:
        steps = jax.random.uniform(jax.random.fold_in(jax.random.fold_in(stream_key, 6), axis_at), (shards_of,), jnp.float32, smallest / len(cuts), high / len(cuts))
        gain = gain * jnp.repeat(jnp.exp(steps), extent[axis_at] // shards_of).reshape((-1,) + (1,) * (len(extent) - 1 - axis_at))
    return gain


def gaussian(stream_key, dims, spread, reach, shards=(), kind=jnp.bfloat16):
    entries = spread * jax.random.normal(stream_key, dims, jnp.float32)
    if shards:
        entries = entries * shard_levels(stream_key, dims, shards, -0.22, 0.18)
    return jnp.clip(entries, -reach, reach).astype(kind)


def setup_inputs(seed: int = 0) -> dict:
    splits = jax.random.split(jax.random.key(seed), 8)
    grad_out = gaussian(splits[0], (NODES, F), 1.0, 6.0, ((0, 128),))
    preact = gaussian(splits[1], (NODES, F), 1.0, 6.0, ((0, 128),))
    features = gaussian(splits[2], (NODES, F), 1.0, 6.0, ((0, 128),))
    weight = gaussian(splits[3], (F, F), F ** -0.5, 0.375)
    adj_values = gaussian(splits[4], (NBR, N_REP * SLOTS, BLOCK, BLOCK), (BLOCK * N_REP * SLOTS // 2) ** -0.5, 0.0625, ((0, 32), (1, 4)))
    adj_cols = draw_adj_cols(jax.random.fold_in(splits[7], 71), 0)
    adj_counts = draw_adj_counts(jax.random.fold_in(splits[7], 71), 0)
    return dict(grad_out=grad_out, preact=preact, features=features, weight=weight, adj_values=adj_values, adj_cols=adj_cols, adj_counts=adj_counts)


def reference(grad_out, preact, features, weight, adj_values, adj_cols, adj_counts):
    grad_pre = jnp.where(preact > 0, grad_out, jnp.zeros_like(grad_out))
    total_rows = adj_values.shape[0]
    slot_total = adj_values.shape[1]
    slot_ids = jnp.arange(slot_total, dtype=jnp.int32)
    counts_per_slot = jnp.take(adj_counts, slot_ids // SLOTS, axis=1)
    alive_slots = ((slot_ids % SLOTS)[None, :] < counts_per_slot).astype(jnp.float32)
    grad_blocks = grad_pre.reshape(total_rows, BLOCK, F)

    def group_step(group, total):
        def row_step(offset, partial_value):
            index = group * ROWBLK + offset
            blocks = adj_values[index].astype(jnp.float32)
            rows_here = grad_blocks[index].astype(jnp.float32)
            messages = jnp.einsum('sij,if->sjf', blocks, rows_here)
            messages = messages * alive_slots[index][:, None, None]
            return partial_value.at[adj_cols[index]].add(messages)

        partial_value = lax.fori_loop(0, ROWBLK, row_step, jnp.zeros((total_rows, BLOCK, F), jnp.float32))
        rounded = lax.optimization_barrier(partial_value.astype(jnp.bfloat16))
        return total + rounded.astype(jnp.float32)

    aggregated = lax.fori_loop(0, N_ROW, group_step, jnp.zeros((total_rows, BLOCK, F), jnp.float32))
    grad_agg = aggregated.reshape(total_rows * BLOCK, F).astype(jnp.bfloat16)
    grad_weight = jnp.dot(features.T, grad_agg, preferred_element_type=jnp.float32)
    grad_features = jnp.dot(grad_agg, weight.T, preferred_element_type=jnp.float32).astype(jnp.bfloat16)
    return grad_features, grad_weight
```

```python
import functools

import jax
import jax.numpy as jnp
import numpy as np
from jax import lax
from jax.experimental import pallas as pl
from jax.experimental.pallas import tpu as pltpu
from jax.sharding import PartitionSpec as P

AXES = ("row", "rep")
RING = 4
BLOCK = 128
FEAT = 256
SHARE_BLOCKS = 4
ROWBLK = 16
SLOTS = 32
CALLS = 8
CALL_SLOTS = 16
MAX_PAIRS = 128
UNROLL = 4
NO_BLOCK = ROWBLK << 9

FLIP = {"x0": ("x", 1), "x1": ("x", 3), "z0": ("z", 1), "z1": ("z", 3), "y0": ("y", 1), "y1": ("y", 3)}
ORDER = (
    (("x0", "z0", "x1", "z1"), ("z0", "x0", "z1", "x1")),
    (("x1", "z1", "x0", "z0"), ("z1", "x1", "z0", "x0")),
)


def linear(z, x, c, y):
    return ((z * RING + x) * 2 + c) * RING + y


def exchange_pairs(first, second):
    pairs = []
    for z in range(RING):
        for x in range(RING):
            for c in range(2):
                for y in range(RING):
                    at = {"z": z, "x": x, "c": c, "y": y}
                    axis, mask = FLIP[first if c == 0 else second]
                    at[axis] ^= mask
                    pairs.append((linear(z, x, c, y), linear(**at)))
    return pairs


def exchange(value, first, second):
    return lax.ppermute(value, AXES, exchange_pairs(first, second))


def swap_cores(value):
    pairs = [(d, d ^ RING) for d in range(RING * RING * 2 * RING)]
    return lax.ppermute(value, AXES, pairs)


def target_flips():
    out = np.zeros((2, 2, 16, 2), np.int32)
    for part in range(2):
        for core in range(2):
            for place in range(16):
                for bit, dim in enumerate(ORDER[part][core]):
                    if place >> (3 - bit) & 1:
                        axis, mask = FLIP[dim]
                        out[part, core, place, 0 if axis == "z" else 1] ^= mask
    return out


def plan(adj_cols, adj_counts, z, x, c, y):
    flips = jnp.asarray(target_flips())
    cores = jnp.stack([c, 1 - c])
    chosen = jnp.where(cores[None, :, None, None] == 0, flips[:, 0][:, None], flips[:, 1][:, None])
    group = ((z ^ chosen[..., 0]) * RING + (x ^ chosen[..., 1])) * 2 + cores[None, :, None]
    base = group * ROWBLK + y * SHARE_BLOCKS + jnp.arange(2, dtype=jnp.int32)[:, None, None] * 2
    target = base[..., None] + jnp.arange(2, dtype=jnp.int32)
    target = target.reshape(CALLS, CALL_SLOTS)

    slot = jnp.arange(SLOTS, dtype=jnp.int32)
    cols = jnp.where(slot[None, :] < adj_counts, adj_cols, -1)
    hit = target[:, :, None, None] == cols
    found = jnp.sum(jnp.where(hit, slot + 1, 0), axis=-1)
    present = (found > 0).astype(jnp.int32)
    row = jnp.arange(ROWBLK, dtype=jnp.int32)
    before = row[:, None] < row[None, :]
    place = jnp.sum(jnp.where(before, present[..., :, None], 0), axis=-2)
    pairs = jnp.maximum((jnp.sum(present, axis=-1) + 1) // 2, 1)
    start = jnp.sum(jnp.where(before, pairs[..., :, None], 0), axis=-2)
    key = jnp.where(present > 0, (start[..., None] + place // 2) * 2 + place % 2, -1)
    step = (row // SHARE_BLOCKS) ^ y
    first = jnp.where(c == 0, 1, 3)
    rel = jnp.where(step == 0, 0, jnp.where(step == first, 1, jnp.where(step == 2, 3, 2)))
    grad = rel * SHARE_BLOCKS + row % SHARE_BLOCKS
    code = row * SLOTS + found - 1 + (grad << 9) - NO_BLOCK
    position = jnp.arange(2 * MAX_PAIRS, dtype=jnp.int32)
    take = key.reshape(CALLS, 1, -1) == position[:, None]
    flat = jnp.sum(jnp.where(take, code.reshape(CALLS, 1, -1), 0), axis=-1) + NO_BLOCK
    pair = jnp.arange(MAX_PAIRS, dtype=jnp.int32)[:, None]
    ended = jnp.sum(((start + pairs)[:, None, :] <= pair).astype(jnp.int32), axis=-1)
    opens = jnp.sum((start[:, None, :] == pair).astype(jnp.int32), axis=-1)
    meta = (jnp.minimum(ended, CALL_SLOTS - 1) + opens * CALL_SLOTS) << 14
    words = flat.reshape(CALLS, MAX_PAIRS, 2) + jnp.stack([meta, jnp.zeros_like(meta)], axis=-1)
    totals = jnp.sum(pairs, axis=-1)
    return words.reshape(-1), totals


def mask_kernel(grad_ref, preact_ref, out_ref):
    for b in range(SHARE_BLOCKS):
        rows = pl.ds(b * BLOCK, BLOCK)
        grad = grad_ref[rows, :].astype(jnp.float32)
        kept = jnp.where(preact_ref[rows, :].astype(jnp.float32) > 0, grad, 0.0)
        out_ref[b] = kept.T.astype(jnp.bfloat16)


def mask(grad_out, preact):
    return pl.pallas_call(
        mask_kernel,
        out_shape=jax.ShapeDtypeStruct((SHARE_BLOCKS, FEAT, BLOCK), jnp.bfloat16),
        compiler_params=pltpu.CompilerParams(vmem_limit_bytes=4 << 20),
        name="masked_gradient",
    )(grad_out, preact)


def products_kernel(call, words_ref, totals_ref, grad_ref, adj_ref, out_ref):
    base = call * 2 * MAX_PAIRS

    def pair(p, acc):
        w0 = words_ref[base + 2 * p]
        w1 = words_ref[base + 2 * p + 1]
        slot = (w0 >> 14) & (CALL_SLOTS - 1)
        keep = jnp.where((w0 >> 18) == 0, 1.0, 0.0).astype(jnp.float32)
        lhs = jnp.concatenate([grad_ref[(w0 >> 9) & 31], grad_ref[(w1 >> 9) & 31]], axis=1)
        rhs = jnp.concatenate([adj_ref[w0 & 511], adj_ref[w1 & 511]], axis=0)
        acc = acc * keep + jnp.dot(lhs, rhs, preferred_element_type=jnp.float32)
        out_ref[slot] = acc.astype(jnp.bfloat16)
        return acc

    def steps(i, acc):
        for u in range(UNROLL):
            acc = pair(i * UNROLL + u, acc)
        return acc

    count = (totals_ref[call] + UNROLL - 1) // UNROLL
    lax.fori_loop(0, count, steps, jnp.zeros((FEAT, BLOCK), jnp.float32))


def products(call, words, totals, grad_t, adj):
    smem = pl.BlockSpec(memory_space=pltpu.SMEM)
    vmem = pl.BlockSpec(memory_space=pltpu.VMEM)
    return pl.pallas_call(
        functools.partial(products_kernel, call),
        out_shape=pltpu.VMEM((CALL_SLOTS, FEAT, BLOCK), jnp.bfloat16),
        in_specs=[smem, smem, vmem, vmem],
        out_specs=vmem,
        cost_estimate=pl.CostEstimate(flops=2 * 48 * 2 * BLOCK * BLOCK * FEAT, bytes_accessed=6 << 20, transcendentals=0),
        compiler_params=pltpu.CompilerParams(vmem_limit_bytes=4 << 20),
        name=f"products_{call}",
    )(
        words,
        totals,
        pltpu.with_memory_space_constraint(grad_t, pltpu.VMEM),
        pltpu.with_memory_space_constraint(adj, pltpu.VMEM),
    )


def add(a, b):
    return (a.astype(jnp.float32) + b.astype(jnp.float32)).astype(jnp.bfloat16)


def body(grad_out, preact, features, weight, adj_values, adj_cols, adj_counts):
    row, y = lax.axis_index("row"), lax.axis_index("rep")
    z, x, c = row // (2 * RING), row // 2 % RING, row % 2

    own = mask(grad_out, preact)
    words, totals = plan(adj_cols, adj_counts, z, x, c, y)
    adj = adj_values.reshape(ROWBLK * SLOTS, BLOCK, BLOCK)

    half = jnp.concatenate([own, exchange(own, "y0", "y1")])
    rest = exchange(half, "y1", "y0")
    grad_t = jnp.concatenate([half, rest, jnp.zeros((1, FEAT, BLOCK), jnp.bfloat16)])

    def product(part, sent, upper):
        return products(part * 4 + sent * 2 + upper, words, totals, grad_t, adj)

    sums = {}
    for upper in (1, 0):
        for part in (0, 1):
            sent = swap_cores(product(part, 1, upper))
            sums[part, upper] = add(product(part, 0, upper), sent)

    parts = []
    for part in (0, 1):
        lower, upper = sums[part, 0], sums[part, 1]
        for step in range(4):
            got = exchange(upper, ORDER[part][0][step], ORDER[part][1][step])
            value = add(lower, got)
            n = value.shape[0] // 2
            if step < 3:
                lower, upper = value[:n], value[n:]
        parts.append(value)
    grad_agg_t = jnp.concatenate(parts)

    feat = features.reshape(SHARE_BLOCKS, BLOCK, FEAT)
    term = jnp.einsum("bfn,bnc->cf", grad_agg_t, feat, preferred_element_type=jnp.float32)
    n = FEAT // 2
    mine = lax.dynamic_slice(term, (c * n, 0), (n, FEAT))
    other = lax.dynamic_slice(term, ((1 - c) * n, 0), (n, FEAT))
    mine = mine + swap_cores(other)
    for dims in (("x0", "z0"), ("z0", "x0"), ("y0", "x1"), ("x1", "y0"), ("z1", "y1"), ("y1", "z1")):
        mine = mine + exchange(mine, *dims)
    theirs = swap_cores(mine)
    low = jnp.where(c == 0, mine, theirs)
    high = jnp.where(c == 0, theirs, mine)
    grad_weight = jnp.concatenate([low, high])

    grad_features = jnp.einsum("bfn,cf->bnc", grad_agg_t, weight, preferred_element_type=jnp.float32)
    return grad_features.astype(jnp.bfloat16).reshape(features.shape), grad_weight


def solution(mesh):
    placed = (
        P(AXES, None),
        P(AXES, None),
        P(AXES, None),
        P(),
        P("row", "rep", None, None),
        P("row", "rep"),
        P("row", "rep"),
    )
    return jax.shard_map(body, mesh=mesh, in_specs=placed, out_specs=(P(AXES, None), P()), check_vma=False)
```

```python
import functools

import jax
import jax.numpy as jnp
from jax import lax
from jax.experimental import pallas as pl
from jax.experimental.pallas import tpu as pltpu
from jax.sharding import PartitionSpec as P

AXES = ("row", "rep")
RING = 4
BLOCK = 128
FEAT = 256
SHARE_BLOCKS = 4
ROWBLK = 16
SLOTS = 32
CALLS = 4
CALL_SLOTS = 32
MAX_PAIRS = 256
UNROLL = 16
AFTER = {1: 2, 3: 3}
NO_BLOCK = ROWBLK << 9

FLIP = {"x0": ("x", 1), "x1": ("x", 3), "z0": ("z", 1), "z1": ("z", 3), "y0": ("y", 1), "y1": ("y", 3)}
ORDER = (
    (("x0", "z0", "x1", "z1"), ("z0", "x0", "z1", "x1")),
    (("x1", "z1", "x0", "z0"), ("z1", "x1", "z0", "x0")),
)


def linear(z, x, c, y):
    return ((z * RING + x) * 2 + c) * RING + y


def exchange_pairs(first, second):
    pairs = []
    for z in range(RING):
        for x in range(RING):
            for c in range(2):
                for y in range(RING):
                    at = {"z": z, "x": x, "c": c, "y": y}
                    axis, mask = FLIP[first if c == 0 else second]
                    at[axis] ^= mask
                    pairs.append((linear(z, x, c, y), linear(**at)))
    return pairs


def exchange(value, first, second):
    return lax.ppermute(value, AXES, exchange_pairs(first, second))


def swap_cores(value):
    pairs = [(d, d ^ RING) for d in range(RING * RING * 2 * RING)]
    return lax.ppermute(value, AXES, pairs)


def prepare_kernel(where_ref, counts_ref, cols_ref, adj_ref, *refs):
    out_ref, words_refs, sem = refs[-CALLS - 2], refs[-CALLS - 1 : -1], refs[-1]

    def copies(action):
        for r in range(ROWBLK):
            count = counts_ref[r]
            for bit in range(6):
                size = 1 << bit
                offset = r * SLOTS + (count & ~(2 * size - 1))

                @pl.when((count & size) != 0)
                def _(offset=offset, size=size):
                    at = pl.ds(offset, size)
                    action(pltpu.make_async_copy(adj_ref.at[at], out_ref.at[at], sem))

    copies(lambda copy: copy.start())
    plan(where_ref, counts_ref, cols_ref, words_refs)
    copies(lambda copy: copy.wait())


def plan(where_ref, counts_ref, cols_ref, words_refs):
    i32 = jnp.int32
    z, x, c, y = (where_ref[i] for i in range(4))
    slots = CALLS * CALL_SLOTS

    lane = lax.broadcasted_iota(i32, (8, slots), 1)
    sent, upper, part = lane >> 6, (lane >> 5) & 1, (lane >> 4) & 1
    core = c ^ sent
    place = upper * 8 + ((lane & 15) >> 1)
    at = {"z": jnp.zeros_like(lane) + z, "x": jnp.zeros_like(lane) + x}
    for bit in range(4):
        on = (place >> (3 - bit)) & 1
        for p in range(2):
            for k in range(2):
                axis, mask = FLIP[ORDER[p][k][bit]]
                at[axis] = at[axis] ^ jnp.where((part == p) & (core == k), on * mask, 0)
    group = (at["z"] * RING + at["x"]) * 2 + core
    target = (group * ROWBLK + y * SHARE_BLOCKS + part * 2 + (lane & 1))[:1]

    index = lax.broadcasted_iota(i32, (ROWBLK, SLOTS), 0)
    live = jnp.zeros((ROWBLK, SLOTS), i32)
    for r in range(ROWBLK):
        live = jnp.where(index == r, counts_ref[r], live)
    cols = jnp.where(lax.broadcasted_iota(i32, (ROWBLK, SLOTS), 1) < live, cols_ref[...], -1)
    found = jnp.zeros((ROWBLK, slots), i32)
    for s in range(SLOTS):
        found = found + jnp.where(cols[:, s : s + 1] == target, s + 1, 0)
    present = jnp.where(found > 0, 1, 0)
    before, count = [], jnp.zeros((1, slots), i32)
    for r in range(ROWBLK):
        before.append(count)
        count = count + present[r : r + 1]
    before = jnp.concatenate(before, axis=0)
    pairs = jnp.maximum((count + 1) >> 1, 1)
    i0 = lax.broadcasted_iota(i32, (slots, slots), 0)
    i1 = lax.broadcasted_iota(i32, (slots, slots), 1)
    earlier = jnp.where((i0 >> 5 == i1 >> 5) & (i0 < i1), 1.0, 0.0).astype(jnp.bfloat16)
    wide = jnp.broadcast_to(pairs, (16, slots)).astype(jnp.float32).astype(jnp.bfloat16)
    start = jnp.dot(wide, earlier, preferred_element_type=jnp.float32).astype(i32)

    key = jnp.where(found > 0, start + (before >> 1) + (before & 1) * MAX_PAIRS, -1)
    row = lax.broadcasted_iota(i32, (ROWBLK, slots), 0)
    step = (row >> 2) ^ y
    first = jnp.where(c == 0, 1, 3)
    rel = jnp.where(step == 0, 0, jnp.where(step == first, 1, jnp.where(step == 2, 3, 2)))
    grad = rel * SHARE_BLOCKS + (row & 3)
    code = row * SLOTS + found - 1 + (grad << 9) - NO_BLOCK

    key_t, code_t, start_t = key.T, code.T, start.T
    end_t = start_t + jnp.broadcast_to(pairs, (16, slots)).T
    position = lax.broadcasted_iota(i32, (CALL_SLOTS, 2 * MAX_PAIRS), 1)
    pair = position[:, :MAX_PAIRS]
    for call in range(CALLS):
        rows = slice(call * CALL_SLOTS, (call + 1) * CALL_SLOTS)
        flat = jnp.zeros((CALL_SLOTS, 2 * MAX_PAIRS), i32)
        for r in range(ROWBLK):
            flat = flat + jnp.where(key_t[rows, r : r + 1] == position, code_t[rows, r : r + 1], 0)
        words = jnp.sum(flat, axis=0, keepdims=True) + NO_BLOCK
        ended = jnp.sum(jnp.where(end_t[rows, :1] <= pair, 1, 0), axis=0, keepdims=True)
        opens = jnp.sum(jnp.where(start_t[rows, :1] == pair, 1, 0), axis=0, keepdims=True)
        meta = (jnp.minimum(ended, CALL_SLOTS - 1) + opens * CALL_SLOTS) << 14
        last = end_t[call * CALL_SLOTS + CALL_SLOTS - 1 : (call + 1) * CALL_SLOTS, :1]
        words_refs[call][:, :MAX_PAIRS] = words[:, :MAX_PAIRS] + meta
        words_refs[call][:, MAX_PAIRS : 2 * MAX_PAIRS] = words[:, MAX_PAIRS:]
        words_refs[call][:, 2 * MAX_PAIRS :] = jnp.broadcast_to(last, (1, BLOCK))

def prepare(adj_values, adj_cols, adj_counts, where, gates):
    shape = (ROWBLK * SLOTS, BLOCK, BLOCK)
    words = pltpu.VMEM((1, 2 * MAX_PAIRS + BLOCK), jnp.int32)
    return pl.pallas_call(
        prepare_kernel,
        out_shape=(pltpu.VMEM(shape, jnp.bfloat16),) + (words,) * CALLS,
        in_specs=[IN_SMEM, IN_SMEM, IN_VMEM, ANYWHERE] + [ANYWHERE] * len(gates),
        out_specs=(IN_VMEM,) * (1 + CALLS),
        scratch_shapes=[pltpu.SemaphoreType.DMA],
        compiler_params=pltpu.CompilerParams(vmem_limit_bytes=4 << 20),
        cost_estimate=TINY,
        name="prepare",
    )(
        where,
        pltpu.with_memory_space_constraint(adj_counts.reshape(-1), pltpu.HBM),
        pltpu.with_memory_space_constraint(adj_cols, pltpu.HBM),
        pltpu.with_memory_space_constraint(adj_values.reshape(shape), pltpu.HBM),
        *gates,
    )


TINY = pl.CostEstimate(flops=0, bytes_accessed=1024, transcendentals=0)
ANYWHERE = pl.BlockSpec(memory_space=pl.ANY)
IN_VMEM = pl.BlockSpec(memory_space=pltpu.VMEM)
IN_SMEM = pl.BlockSpec(memory_space=pltpu.SMEM)


def in_vmem(value):
    return pltpu.with_memory_space_constraint(value, pltpu.VMEM)


def load_kernel(grad_ref, preact_ref, feat_ref, own_ref, feat0_ref, feat1_ref, grad, preact, sems):
    first = pltpu.make_async_copy(grad_ref, grad, sems.at[0])
    second = pltpu.make_async_copy(preact_ref, preact, sems.at[1])
    third = pltpu.make_async_copy(feat_ref.at[pl.ds(0, 2)], feat0_ref, sems.at[2])
    fourth = pltpu.make_async_copy(feat_ref.at[pl.ds(2, 2)], feat1_ref, sems.at[3])
    copies = (first, second, third, fourth)
    for copy in copies:
        copy.start()
    for copy in copies:
        copy.wait()
    for b in range(SHARE_BLOCKS):
        value = grad[b].astype(jnp.float32)
        own_ref[b] = jnp.where(preact[b].astype(jnp.float32) > 0, value, 0.0).astype(jnp.bfloat16)


def load(grad_out, preact, features):
    whole, part = (SHARE_BLOCKS, BLOCK, FEAT), (2, BLOCK, FEAT)
    return pl.pallas_call(
        load_kernel,
        out_shape=tuple(pltpu.VMEM(s, jnp.bfloat16) for s in (whole, part, part)),
        in_specs=[ANYWHERE] * 3,
        out_specs=(IN_VMEM,) * 3,
        scratch_shapes=[pltpu.VMEM(whole, jnp.bfloat16)] * 2 + [pltpu.SemaphoreType.DMA((4,))],
        compiler_params=pltpu.CompilerParams(vmem_limit_bytes=4 << 20),
        cost_estimate=TINY,
        name="load",
    )(*(pltpu.with_memory_space_constraint(v.reshape(whole), pltpu.HBM) for v in (grad_out, preact, features)))


def join_kernel(n, *refs):
    out_ref = refs[-1]
    at = 0
    for ref in refs[:n]:
        size = ref.shape[0]
        out_ref[at : at + size] = ref[...]
        at += size
    if at < out_ref.shape[0]:
        out_ref[at:] = jnp.zeros_like(out_ref[at:])


def join(pieces, gates=(), zeros=0):
    size = sum(p.shape[0] for p in pieces) + zeros
    return pl.pallas_call(
        functools.partial(join_kernel, len(pieces)),
        out_shape=pltpu.VMEM((size, *pieces[0].shape[1:]), pieces[0].dtype),
        in_specs=[IN_VMEM] * len(pieces) + [ANYWHERE] * len(gates),
        out_specs=IN_VMEM,
        compiler_params=pltpu.CompilerParams(vmem_limit_bytes=4 << 20),
        cost_estimate=TINY,
        name="join",
    )(*(in_vmem(p) for p in pieces), *gates)


def fold_kernel(n, kept_ref, got_ref, *refs):
    at = 0
    for ref in refs[-n:]:
        size = ref.shape[0]
        for b in range(size):
            ref[b] = (kept_ref[at + b].astype(jnp.float32) + got_ref[at + b].astype(jnp.float32)).astype(jnp.bfloat16)
        at += size


def fold(kept, got, halves, gates=()):
    size, *rest = kept.shape
    out = tuple(pltpu.VMEM((size // halves, *rest), jnp.bfloat16) for _ in range(halves))
    return pl.pallas_call(
        functools.partial(fold_kernel, halves),
        out_shape=out,
        in_specs=[IN_VMEM] * 2 + [ANYWHERE] * len(gates),
        out_specs=(IN_VMEM,) * halves,
        compiler_params=pltpu.CompilerParams(vmem_limit_bytes=4 << 20),
        cost_estimate=TINY,
        name="fold",
    )(in_vmem(kept), in_vmem(got), *gates)


def features_kernel(first_ref, second_ref, weight_ref, out_ref):
    for k, ref in enumerate((first_ref, second_ref)):
        for b in range(2):
            rows = pl.ds((2 * k + b) * BLOCK, BLOCK)
            value = lax.dot_general(
                ref[b], weight_ref[...], (((1,), (1,)), ((), ())), preferred_element_type=jnp.float32
            )
            out_ref[rows, :] = value.astype(jnp.bfloat16)


def features_gradient(first, second, weight):
    return pl.pallas_call(
        features_kernel,
        out_shape=jax.ShapeDtypeStruct((SHARE_BLOCKS * BLOCK, FEAT), jnp.bfloat16),
        in_specs=[IN_VMEM] * 3,
        out_specs=IN_VMEM,
        compiler_params=pltpu.CompilerParams(vmem_limit_bytes=4 << 20),
        cost_estimate=TINY,
        name="features_gradient",
    )(in_vmem(first), in_vmem(second), weight)


def weight_kernel(core_ref, *refs):
    ins, outs = refs[:-2], refs[-2:]
    n = FEAT // 2
    for k, out_ref in enumerate(outs):
        rows = pl.ds(pl.multiple_of((core_ref[0] ^ k) * n, n), n)
        total = jnp.zeros((n, FEAT), jnp.float32)
        for feat, held in zip(ins[::2], ins[1::2]):
            size = feat.shape[0] * BLOCK
            left = feat[:, :, rows].reshape(size, n)
            total = total + lax.dot_general(
                left, held[...].reshape(size, FEAT), (((0,), (0,)), ((), ())), preferred_element_type=jnp.float32
            )
        out_ref[...] = total.astype(out_ref.dtype)


def weight_terms(core, pairs):
    flat = [in_vmem(v) for pair in pairs for v in pair]
    return pl.pallas_call(
        weight_kernel,
        out_shape=tuple(pltpu.VMEM((FEAT // 2, FEAT), t) for t in (jnp.float32, jnp.bfloat16)),
        in_specs=[IN_SMEM] + [IN_VMEM] * len(flat),
        out_specs=(IN_VMEM,) * 2,
        compiler_params=pltpu.CompilerParams(vmem_limit_bytes=8 << 20),
        cost_estimate=TINY,
        name="weight_terms",
    )(core.reshape(1), *flat)


def products_kernel(words_ref, grad_ref, adj_ref, *refs):
    out_ref = refs[-1]

    def pair(p, acc):
        w0 = words_ref[0, p]
        w1 = words_ref[0, MAX_PAIRS + p]
        slot = (w0 >> 14) & (CALL_SLOTS - 1)
        keep = jnp.where((w0 >> 19) == 0, 1.0, 0.0).astype(jnp.float32)
        grad = jnp.concatenate([grad_ref[(w0 >> 9) & 31], grad_ref[(w1 >> 9) & 31]], axis=0)
        adj = jnp.concatenate([adj_ref[w0 & 511], adj_ref[w1 & 511]], axis=0)
        term = lax.dot_general(adj, grad, (((0,), (0,)), ((), ())), preferred_element_type=jnp.float32)
        acc = acc * keep + term
        out_ref[slot] = acc.astype(jnp.bfloat16)
        return acc

    def steps(i, acc):
        for u in range(UNROLL):
            acc = pair(i * UNROLL + u, acc)
        return acc

    count = (words_ref[0, 2 * MAX_PAIRS] + UNROLL - 1) // UNROLL
    lax.fori_loop(0, count, steps, jnp.zeros((BLOCK, FEAT), jnp.float32))


def products(name, words, grad, adj, gates):
    return pl.pallas_call(
        products_kernel,
        out_shape=pltpu.VMEM((CALL_SLOTS, BLOCK, FEAT), jnp.bfloat16),
        in_specs=[IN_SMEM, IN_VMEM, IN_VMEM] + [ANYWHERE] * len(gates),
        out_specs=IN_VMEM,
        compiler_params=pltpu.CompilerParams(vmem_limit_bytes=4 << 20),
        cost_estimate=TINY,
        name=f"products_{name}",
    )(
        words,
        in_vmem(grad),
        in_vmem(adj),
        *gates,
    )


def body(grad_out, preact, features, weight, adj_values, adj_cols, adj_counts):
    row, y = lax.axis_index("row"), lax.axis_index("rep")
    z, x, c = row // (2 * RING), row // 2 % RING, row % 2
    core = c.astype(jnp.int32)

    own, *mine = load(grad_out, preact, features)
    got = exchange(own, "y0", "y1")
    near = [exchange(mine[p], ORDER[p][0][3], ORDER[p][1][3]) for p in (0, 1)]
    half = join([own, got], near)
    got = exchange(half, "y1", "y0")
    feats = [join([mine[p], near[p]], [half]) for p in (0, 1)]
    far = [exchange(feats[p], ORDER[p][0][2], ORDER[p][1][2]) for p in (0, 1)]
    where = jnp.stack([z, x, c, y]).astype(jnp.int32)
    adj, *words = prepare(adj_values, adj_cols, adj_counts, where, feats)
    grad = join([half, got], [adj, *far], zeros=1)

    def product(sent, upper, gates=()):
        call = sent * 2 + upper
        return products(call, words[call], grad, adj, gates)

    sent_upper = product(1, 1)
    sent_lower = product(1, 0, [sent_upper])
    kept_upper = product(0, 1, [sent_lower])
    upper = list(fold(kept_upper, swap_cores(sent_upper), 2))
    kept_lower = product(0, 0, upper)
    lower = list(fold(kept_lower, swap_cores(sent_lower), 2))

    def halve(step, gates=()):
        for p in (0, 1):
            got = exchange(upper[p], ORDER[p][0][step], ORDER[p][1][step])
            lower[p], *rest = fold(lower[p], got, 2 if step < 3 else 1, gates)
            upper[p] = rest[0] if rest else None
        return list(lower)

    halve(0)
    halve(1)
    held = [(v[p], w[p]) for p in (0, 1) for v, w in ((feats, lower), (far, upper))]
    term, other = weight_terms(core, held)
    (term,) = fold(term, swap_cores(other), 1)
    for k, dims in enumerate((("y0", "y1"), ("y1", "y0"), ("x0", "z0"), ("z0", "x0"), ("x1", "z1"), ("z1", "x1"))):
        got = exchange(term, *dims)
        gates = halve(AFTER[k], [term]) if k in AFTER else ()
        (term,) = fold(term, got, 1, gates)
    theirs = swap_cores(term)
    grad_weight = jnp.concatenate([jnp.where(c == 0, term, theirs), jnp.where(c == 0, theirs, term)])
    return features_gradient(*lower, weight), grad_weight.astype(jnp.float32)


def solution(mesh):
    placed = (
        P(AXES, None),
        P(AXES, None),
        P(AXES, None),
        P(),
        P("row", "rep", None, None),
        P("row", "rep"),
        P("row", "rep"),
    )
    return jax.shard_map(body, mesh=mesh, in_specs=placed, out_specs=(P(AXES, None), P()), check_vma=False)
```

```python
import functools

import jax
import jax.numpy as jnp
from jax import lax
from jax.experimental import pallas as pl
from jax.experimental.pallas import tpu as pltpu
from jax.sharding import PartitionSpec as P

AXES = ("row", "rep")
RING = 4
BLOCK = 128
FEAT = 256
SHARE_BLOCKS = 4
ROWBLK = 16
SLOTS = 32
CALLS = 4
CALL_SLOTS = 32
MAX_PAIRS = 256
UNROLL = 16
NO_BLOCK = ROWBLK << 9

FLIP = {"x0": ("x", 1), "x1": ("x", 3), "z0": ("z", 1), "z1": ("z", 3), "y0": ("y", 1), "y1": ("y", 3)}
ORDER = (
    (("x0", "z0", "x1", "z1"), ("z0", "x0", "z1", "x1")),
    (("x1", "z1", "x0", "z0"), ("z1", "x1", "z0", "x0")),
)


def linear(z, x, c, y):
    return ((z * RING + x) * 2 + c) * RING + y


def exchange_pairs(first, second):
    pairs = []
    for z in range(RING):
        for x in range(RING):
            for c in range(2):
                for y in range(RING):
                    at = {"z": z, "x": x, "c": c, "y": y}
                    axis, mask = FLIP[first if c == 0 else second]
                    at[axis] ^= mask
                    pairs.append((linear(z, x, c, y), linear(**at)))
    return pairs


def exchange(value, first, second):
    return lax.ppermute(value, AXES, exchange_pairs(first, second))


def shift(value, first, second, hops):
    pairs = []
    for z in range(RING):
        for x in range(RING):
            for c in range(2):
                for y in range(RING):
                    at = {"z": z, "x": x, "c": c, "y": y}
                    axis = first if c == 0 else second
                    at[axis] = (at[axis] + hops) % RING
                    pairs.append((linear(z, x, c, y), linear(**at)))
    return lax.ppermute(value, AXES, pairs)


def swap_cores(value):
    pairs = [(d, d ^ RING) for d in range(RING * RING * 2 * RING)]
    return lax.ppermute(value, AXES, pairs)


def prepare_kernel(where_ref, counts_ref, cols_ref, adj_ref, *refs):
    out_ref, words_refs, sem = refs[-CALLS - 2], refs[-CALLS - 1 : -1], refs[-1]

    def copies(action):
        for r in range(ROWBLK):
            count = counts_ref[r]
            for bit in range(6):
                size = 1 << bit
                offset = r * SLOTS + (count & ~(2 * size - 1))

                @pl.when((count & size) != 0)
                def _(offset=offset, size=size):
                    at = pl.ds(offset, size)
                    action(pltpu.make_async_copy(adj_ref.at[at], out_ref.at[at], sem))

    copies(lambda copy: copy.start())
    plan(where_ref, counts_ref, cols_ref, words_refs)
    copies(lambda copy: copy.wait())


def plan(where_ref, counts_ref, cols_ref, words_refs):
    i32 = jnp.int32
    z, x, c, y = (where_ref[i] for i in range(4))
    slots = CALLS * CALL_SLOTS

    lane = lax.broadcasted_iota(i32, (8, slots), 1)
    sent, upper, part = lane >> 6, (lane >> 5) & 1, (lane >> 4) & 1
    core = c ^ sent
    place = upper * 8 + ((lane & 15) >> 1)
    at = {"z": jnp.zeros_like(lane) + z, "x": jnp.zeros_like(lane) + x}
    for bit in range(4):
        on = (place >> (3 - bit)) & 1
        for p in range(2):
            for k in range(2):
                axis, mask = FLIP[ORDER[p][k][bit]]
                at[axis] = at[axis] ^ jnp.where((part == p) & (core == k), on * mask, 0)
    group = (at["z"] * RING + at["x"]) * 2 + core
    target = (group * ROWBLK + y * SHARE_BLOCKS + part * 2 + (lane & 1))[:1]

    index = lax.broadcasted_iota(i32, (ROWBLK, SLOTS), 0)
    live = jnp.zeros((ROWBLK, SLOTS), i32)
    for r in range(ROWBLK):
        live = jnp.where(index == r, counts_ref[r], live)
    cols = jnp.where(lax.broadcasted_iota(i32, (ROWBLK, SLOTS), 1) < live, cols_ref[...], -1)
    found = jnp.zeros((ROWBLK, slots), i32)
    for s in range(SLOTS):
        found = found + jnp.where(cols[:, s : s + 1] == target, s + 1, 0)
    present = jnp.where(found > 0, 1, 0)
    before, count = [], jnp.zeros((1, slots), i32)
    for r in range(ROWBLK):
        before.append(count)
        count = count + present[r : r + 1]
    before = jnp.concatenate(before, axis=0)
    pairs = jnp.maximum((count + 1) >> 1, 1)
    i0 = lax.broadcasted_iota(i32, (slots, slots), 0)
    i1 = lax.broadcasted_iota(i32, (slots, slots), 1)
    earlier = jnp.where((i0 >> 5 == i1 >> 5) & (i0 < i1), 1.0, 0.0).astype(jnp.bfloat16)
    wide = jnp.broadcast_to(pairs, (16, slots)).astype(jnp.float32).astype(jnp.bfloat16)
    start = jnp.dot(wide, earlier, preferred_element_type=jnp.float32).astype(i32)

    key = jnp.where(found > 0, start + (before >> 1) + (before & 1) * MAX_PAIRS, -1)
    row = lax.broadcasted_iota(i32, (ROWBLK, slots), 0)
    step = (row >> 2) ^ y
    first = jnp.where(c == 0, 1, 3)
    rel = jnp.where(step == 0, 0, jnp.where(step == first, 1, jnp.where(step == 2, 3, 2)))
    grad = rel * SHARE_BLOCKS + (row & 3)
    code = row * SLOTS + found - 1 + (grad << 9) - NO_BLOCK

    key_t, code_t, start_t = key.T, code.T, start.T
    end_t = start_t + jnp.broadcast_to(pairs, (16, slots)).T
    position = lax.broadcasted_iota(i32, (CALL_SLOTS, 2 * MAX_PAIRS), 1)
    pair = position[:, :MAX_PAIRS]
    for call in range(CALLS):
        rows = slice(call * CALL_SLOTS, (call + 1) * CALL_SLOTS)
        flat = jnp.zeros((CALL_SLOTS, 2 * MAX_PAIRS), i32)
        for r in range(ROWBLK):
            flat = flat + jnp.where(key_t[rows, r : r + 1] == position, code_t[rows, r : r + 1], 0)
        words = jnp.sum(flat, axis=0, keepdims=True) + NO_BLOCK
        ended = jnp.sum(jnp.where(end_t[rows, :1] <= pair, 1, 0), axis=0, keepdims=True)
        opens = jnp.sum(jnp.where(start_t[rows, :1] == pair, 1, 0), axis=0, keepdims=True)
        meta = (jnp.minimum(ended, CALL_SLOTS - 1) + opens * CALL_SLOTS) << 14
        last = end_t[call * CALL_SLOTS + CALL_SLOTS - 1 : (call + 1) * CALL_SLOTS, :1]
        words_refs[call][:, :MAX_PAIRS] = words[:, :MAX_PAIRS] + meta
        words_refs[call][:, MAX_PAIRS : 2 * MAX_PAIRS] = words[:, MAX_PAIRS:]
        words_refs[call][:, 2 * MAX_PAIRS :] = jnp.broadcast_to(last, (1, BLOCK))

def prepare(adj_values, adj_cols, adj_counts, where, gates):
    shape = (ROWBLK * SLOTS, BLOCK, BLOCK)
    words = pltpu.VMEM((1, 2 * MAX_PAIRS + BLOCK), jnp.int32)
    return pl.pallas_call(
        prepare_kernel,
        out_shape=(pltpu.VMEM(shape, jnp.bfloat16),) + (words,) * CALLS,
        in_specs=[IN_SMEM, IN_SMEM, IN_VMEM, ANYWHERE] + [ANYWHERE] * len(gates),
        out_specs=(IN_VMEM,) * (1 + CALLS),
        scratch_shapes=[pltpu.SemaphoreType.DMA],
        compiler_params=pltpu.CompilerParams(vmem_limit_bytes=4 << 20),
        cost_estimate=TINY,
        name="prepare",
    )(
        where,
        pltpu.with_memory_space_constraint(adj_counts.reshape(-1), pltpu.HBM),
        pltpu.with_memory_space_constraint(adj_cols, pltpu.HBM),
        pltpu.with_memory_space_constraint(adj_values.reshape(shape), pltpu.HBM),
        *gates,
    )


TINY = pl.CostEstimate(flops=0, bytes_accessed=1024, transcendentals=0)
ANYWHERE = pl.BlockSpec(memory_space=pl.ANY)
IN_VMEM = pl.BlockSpec(memory_space=pltpu.VMEM)
IN_SMEM = pl.BlockSpec(memory_space=pltpu.SMEM)


def in_vmem(value):
    return pltpu.with_memory_space_constraint(value, pltpu.VMEM)


def load_kernel(grad_ref, preact_ref, feat_ref, own_ref, feat0_ref, feat1_ref, grad, preact, sems):
    first = pltpu.make_async_copy(grad_ref, grad, sems.at[0])
    second = pltpu.make_async_copy(preact_ref, preact, sems.at[1])
    third = pltpu.make_async_copy(feat_ref.at[pl.ds(0, 2)], feat0_ref, sems.at[2])
    fourth = pltpu.make_async_copy(feat_ref.at[pl.ds(2, 2)], feat1_ref, sems.at[3])
    copies = (first, second, third, fourth)
    for copy in copies:
        copy.start()
    for copy in copies:
        copy.wait()
    for b in range(SHARE_BLOCKS):
        value = grad[b].astype(jnp.float32)
        own_ref[b] = jnp.where(preact[b].astype(jnp.float32) > 0, value, 0.0).astype(jnp.bfloat16)


def load(grad_out, preact, features):
    whole, part = (SHARE_BLOCKS, BLOCK, FEAT), (2, BLOCK, FEAT)
    return pl.pallas_call(
        load_kernel,
        out_shape=tuple(pltpu.VMEM(s, jnp.bfloat16) for s in (whole, part, part)),
        in_specs=[ANYWHERE] * 3,
        out_specs=(IN_VMEM,) * 3,
        scratch_shapes=[pltpu.VMEM(whole, jnp.bfloat16)] * 2 + [pltpu.SemaphoreType.DMA((4,))],
        compiler_params=pltpu.CompilerParams(vmem_limit_bytes=4 << 20),
        cost_estimate=TINY,
        name="load",
    )(*(pltpu.with_memory_space_constraint(v.reshape(whole), pltpu.HBM) for v in (grad_out, preact, features)))


def join_kernel(n, *refs):
    out_ref = refs[-1]
    at = 0
    for ref in refs[:n]:
        size = ref.shape[0]
        out_ref[at : at + size] = ref[...]
        at += size
    if at < out_ref.shape[0]:
        out_ref[at:] = jnp.zeros_like(out_ref[at:])


def join(pieces, gates=(), zeros=0):
    size = sum(p.shape[0] for p in pieces) + zeros
    return pl.pallas_call(
        functools.partial(join_kernel, len(pieces)),
        out_shape=pltpu.VMEM((size, *pieces[0].shape[1:]), pieces[0].dtype),
        in_specs=[IN_VMEM] * len(pieces) + [ANYWHERE] * len(gates),
        out_specs=IN_VMEM,
        compiler_params=pltpu.CompilerParams(vmem_limit_bytes=4 << 20),
        cost_estimate=TINY,
        name="join",
    )(*(in_vmem(p) for p in pieces), *gates)


def fold_kernel(n, kept_ref, got_ref, *refs):
    at = 0
    for ref in refs[-n:]:
        size = ref.shape[0]
        for b in range(size):
            ref[b] = (kept_ref[at + b].astype(jnp.float32) + got_ref[at + b].astype(jnp.float32)).astype(jnp.bfloat16)
        at += size


def fold(kept, got, halves, gates=()):
    size, *rest = kept.shape
    out = tuple(pltpu.VMEM((size // halves, *rest), jnp.bfloat16) for _ in range(halves))
    return pl.pallas_call(
        functools.partial(fold_kernel, halves),
        out_shape=out,
        in_specs=[IN_VMEM] * 2 + [ANYWHERE] * len(gates),
        out_specs=(IN_VMEM,) * halves,
        compiler_params=pltpu.CompilerParams(vmem_limit_bytes=4 << 20),
        cost_estimate=TINY,
        name="fold",
    )(in_vmem(kept), in_vmem(got), *gates)


def ring_kernel(own_ref, opposite_ref, left_ref, right_ref, *refs):
    own, opposite, left, right = (
        r[...].astype(jnp.float32) for r in (own_ref, opposite_ref, left_ref, right_ref)
    )
    refs[-1][...] = ((own + opposite) + (left + right)).astype(jnp.bfloat16)


def ring_sum(own, got, gates=()):
    return pl.pallas_call(
        ring_kernel,
        out_shape=pltpu.VMEM(own.shape, jnp.bfloat16),
        in_specs=[IN_VMEM] * 4 + [ANYWHERE] * len(gates),
        out_specs=IN_VMEM,
        compiler_params=pltpu.CompilerParams(vmem_limit_bytes=4 << 20),
        cost_estimate=TINY,
        name="ring_sum",
    )(in_vmem(own), *(in_vmem(v) for v in got), *gates)


def features_kernel(first_ref, second_ref, weight_ref, out_ref):
    for k, ref in enumerate((first_ref, second_ref)):
        for b in range(2):
            rows = pl.ds((2 * k + b) * BLOCK, BLOCK)
            value = lax.dot_general(
                ref[b], weight_ref[...], (((1,), (1,)), ((), ())), preferred_element_type=jnp.float32
            )
            out_ref[rows, :] = value.astype(jnp.bfloat16)


def features_gradient(first, second, weight):
    return pl.pallas_call(
        features_kernel,
        out_shape=jax.ShapeDtypeStruct((SHARE_BLOCKS * BLOCK, FEAT), jnp.bfloat16),
        in_specs=[IN_VMEM] * 3,
        out_specs=IN_VMEM,
        compiler_params=pltpu.CompilerParams(vmem_limit_bytes=4 << 20),
        cost_estimate=TINY,
        name="features_gradient",
    )(in_vmem(first), in_vmem(second), weight)


def weight_kernel(core_ref, *refs):
    ins, outs = refs[:-2], refs[-2:]
    n = FEAT // 2
    for k, out_ref in enumerate(outs):
        rows = pl.ds(pl.multiple_of((core_ref[0] ^ k) * n, n), n)
        total = jnp.zeros((n, FEAT), jnp.float32)
        for feat, held in zip(ins[::2], ins[1::2]):
            size = feat.shape[0] * BLOCK
            left = feat[:, :, rows].reshape(size, n)
            total = total + lax.dot_general(
                left, held[...].reshape(size, FEAT), (((0,), (0,)), ((), ())), preferred_element_type=jnp.float32
            )
        out_ref[...] = total.astype(out_ref.dtype)


def weight_terms(core, pairs):
    flat = [in_vmem(v) for pair in pairs for v in pair]
    return pl.pallas_call(
        weight_kernel,
        out_shape=tuple(pltpu.VMEM((FEAT // 2, FEAT), t) for t in (jnp.float32, jnp.bfloat16)),
        in_specs=[IN_SMEM] + [IN_VMEM] * len(flat),
        out_specs=(IN_VMEM,) * 2,
        compiler_params=pltpu.CompilerParams(vmem_limit_bytes=8 << 20),
        cost_estimate=TINY,
        name="weight_terms",
    )(core.reshape(1), *flat)


def products_kernel(words_ref, grad_ref, adj_ref, *refs):
    out_ref = refs[-1]

    def pair(p, acc):
        w0 = words_ref[0, p]
        w1 = words_ref[0, MAX_PAIRS + p]
        slot = (w0 >> 14) & (CALL_SLOTS - 1)
        keep = jnp.where((w0 >> 19) == 0, 1.0, 0.0).astype(jnp.float32)
        grad = jnp.concatenate([grad_ref[(w0 >> 9) & 31], grad_ref[(w1 >> 9) & 31]], axis=0)
        adj = jnp.concatenate([adj_ref[w0 & 511], adj_ref[w1 & 511]], axis=0)
        term = lax.dot_general(adj, grad, (((0,), (0,)), ((), ())), preferred_element_type=jnp.float32)
        acc = acc * keep + term
        out_ref[slot] = acc.astype(jnp.bfloat16)
        return acc

    def steps(i, acc):
        for u in range(UNROLL):
            acc = pair(i * UNROLL + u, acc)
        return acc

    count = (words_ref[0, 2 * MAX_PAIRS] + UNROLL - 1) // UNROLL
    lax.fori_loop(0, count, steps, jnp.zeros((BLOCK, FEAT), jnp.float32))


def products(name, words, grad, adj, gates):
    return pl.pallas_call(
        products_kernel,
        out_shape=pltpu.VMEM((CALL_SLOTS, BLOCK, FEAT), jnp.bfloat16),
        in_specs=[IN_SMEM, IN_VMEM, IN_VMEM] + [ANYWHERE] * len(gates),
        out_specs=IN_VMEM,
        compiler_params=pltpu.CompilerParams(vmem_limit_bytes=4 << 20),
        cost_estimate=TINY,
        name=f"products_{name}",
    )(
        words,
        in_vmem(grad),
        in_vmem(adj),
        *gates,
    )


def body(grad_out, preact, features, weight, adj_values, adj_cols, adj_counts):
    row, y = lax.axis_index("row"), lax.axis_index("rep")
    z, x, c = row // (2 * RING), row // 2 % RING, row % 2
    core = c.astype(jnp.int32)

    own, *mine = load(grad_out, preact, features)
    got = exchange(own, "y0", "y1")
    near = [exchange(mine[p], ORDER[p][0][3], ORDER[p][1][3]) for p in (0, 1)]
    half = join([own, got], near)
    got = exchange(half, "y1", "y0")
    feats = [join([mine[p], near[p]], [half]) for p in (0, 1)]
    far = [exchange(feats[p], ORDER[p][0][2], ORDER[p][1][2]) for p in (0, 1)]
    where = jnp.stack([z, x, c, y]).astype(jnp.int32)
    adj, *words = prepare(adj_values, adj_cols, adj_counts, where, feats)
    grad = join([half, got], [adj, *far], zeros=1)

    def product(sent, upper, gates=()):
        call = sent * 2 + upper
        return products(call, words[call], grad, adj, gates)

    sent_upper = product(1, 1)
    sent_lower = product(1, 0, [sent_upper])
    kept_upper = product(0, 1, [sent_lower])
    upper = list(fold(kept_upper, swap_cores(sent_upper), 2))
    kept_lower = product(0, 0, upper)
    lower = list(fold(kept_lower, swap_cores(sent_lower), 2))

    def halve(step, gates=()):
        for p in (0, 1):
            got = exchange(upper[p], ORDER[p][0][step], ORDER[p][1][step])
            lower[p], *rest = fold(lower[p], got, 2 if step < 3 else 1, gates)
            upper[p] = rest[0] if rest else None
        return list(lower)

    halve(0)
    halve(1)
    held = [(v[p], w[p]) for p in (0, 1) for v, w in ((feats, lower), (far, upper))]
    term, other = weight_terms(core, held)
    (term,) = fold(term, swap_cores(other), 1)
    for k, rings in enumerate((("x", "z"), ("z", "x"), ("y", "y"))):
        got = [shift(term, *rings, hops) for hops in (2, 1, 3)]
        term = ring_sum(term, got, lower)
        if k < 2:
            halve(2 + k, [term])
    theirs = swap_cores(term)
    grad_weight = jnp.concatenate([jnp.where(c == 0, term, theirs), jnp.where(c == 0, theirs, term)])
    return features_gradient(*lower, weight), grad_weight.astype(jnp.float32)


def solution(mesh):
    placed = (
        P(AXES, None),
        P(AXES, None),
        P(AXES, None),
        P(),
        P("row", "rep", None, None),
        P("row", "rep"),
        P("row", "rep"),
    )
    return jax.shard_map(body, mesh=mesh, in_specs=placed, out_specs=(P(AXES, None), P()), check_vma=False)
```

```python
import functools

import jax
import jax.numpy as jnp
from jax import lax
from jax.experimental import pallas as pl
from jax.experimental.pallas import tpu as pltpu
from jax.sharding import PartitionSpec as P

AXES = ("row", "rep")
RING = 4
BLOCK = 128
FEAT = 256
SHARE_BLOCKS = 4
ROWBLK = 16
SLOTS = 32
CALLS = 4
CALL_SLOTS = 32
MAX_PAIRS = 256
UNROLL = 16
NO_BLOCK = ROWBLK << 9

FLIP = {"x0": ("x", 1), "x1": ("x", 3), "z0": ("z", 1), "z1": ("z", 3), "y0": ("y", 1), "y1": ("y", 3)}
ORDER = (
    (("x0", "z0", "x1", "z1"), ("z0", "x0", "z1", "x1")),
    (("x1", "z1", "x0", "z0"), ("z1", "x1", "z0", "x0")),
)


def linear(z, x, c, y):
    return ((z * RING + x) * 2 + c) * RING + y


def exchange_pairs(first, second):
    pairs = []
    for z in range(RING):
        for x in range(RING):
            for c in range(2):
                for y in range(RING):
                    at = {"z": z, "x": x, "c": c, "y": y}
                    axis, mask = FLIP[first if c == 0 else second]
                    at[axis] ^= mask
                    pairs.append((linear(z, x, c, y), linear(**at)))
    return pairs


def exchange(value, first, second):
    return lax.ppermute(value, AXES, exchange_pairs(first, second))


def shift(value, first, second, hops):
    pairs = []
    for z in range(RING):
        for x in range(RING):
            for c in range(2):
                for y in range(RING):
                    at = {"z": z, "x": x, "c": c, "y": y}
                    axis = first if c == 0 else second
                    at[axis] = (at[axis] + hops) % RING
                    pairs.append((linear(z, x, c, y), linear(**at)))
    return lax.ppermute(value, AXES, pairs)


def swap_cores(value):
    pairs = [(d, d ^ RING) for d in range(RING * RING * 2 * RING)]
    return lax.ppermute(value, AXES, pairs)


def prepare_kernel(where_ref, counts_ref, cols_ref, adj_ref, *refs):
    out_ref, words_refs, sem = refs[-CALLS - 2], refs[-CALLS - 1 : -1], refs[-1]

    def copies(action):
        for r in range(ROWBLK):
            count = counts_ref[r]
            for bit in range(6):
                size = 1 << bit
                offset = r * SLOTS + (count & ~(2 * size - 1))

                @pl.when((count & size) != 0)
                def _(offset=offset, size=size):
                    at = pl.ds(offset, size)
                    action(pltpu.make_async_copy(adj_ref.at[at], out_ref.at[at], sem))

    copies(lambda copy: copy.start())
    plan(where_ref, counts_ref, cols_ref, words_refs)
    copies(lambda copy: copy.wait())


def plan(where_ref, counts_ref, cols_ref, words_refs):
    i32 = jnp.int32
    z, x, c, y = (where_ref[i] for i in range(4))
    slots = CALLS * CALL_SLOTS

    lane = lax.broadcasted_iota(i32, (8, slots), 1)
    sent, upper, part = lane >> 6, (lane >> 5) & 1, (lane >> 4) & 1
    core = c ^ sent
    place = upper * 8 + ((lane & 15) >> 1)
    at = {"z": jnp.zeros_like(lane) + z, "x": jnp.zeros_like(lane) + x}
    for bit in range(4):
        on = (place >> (3 - bit)) & 1
        for p in range(2):
            for k in range(2):
                axis, mask = FLIP[ORDER[p][k][bit]]
                at[axis] = at[axis] ^ jnp.where((part == p) & (core == k), on * mask, 0)
    group = (at["z"] * RING + at["x"]) * 2 + core
    target = (group * ROWBLK + y * SHARE_BLOCKS + part * 2 + (lane & 1))[:1]

    index = lax.broadcasted_iota(i32, (ROWBLK, SLOTS), 0)
    live = jnp.zeros((ROWBLK, SLOTS), i32)
    for r in range(ROWBLK):
        live = jnp.where(index == r, counts_ref[r], live)
    cols = jnp.where(lax.broadcasted_iota(i32, (ROWBLK, SLOTS), 1) < live, cols_ref[...], -1)
    found = jnp.zeros((ROWBLK, slots), i32)
    for s in range(SLOTS):
        found = found + jnp.where(cols[:, s : s + 1] == target, s + 1, 0)
    present = jnp.where(found > 0, 1, 0)
    before, count = [], jnp.zeros((1, slots), i32)
    for r in range(ROWBLK):
        before.append(count)
        count = count + present[r : r + 1]
    before = jnp.concatenate(before, axis=0)
    pairs = jnp.maximum((count + 1) >> 1, 1)
    i0 = lax.broadcasted_iota(i32, (slots, slots), 0)
    i1 = lax.broadcasted_iota(i32, (slots, slots), 1)
    earlier = jnp.where((i0 >> 5 == i1 >> 5) & (i0 < i1), 1.0, 0.0).astype(jnp.bfloat16)
    wide = jnp.broadcast_to(pairs, (16, slots)).astype(jnp.float32).astype(jnp.bfloat16)
    start = jnp.dot(wide, earlier, preferred_element_type=jnp.float32).astype(i32)

    key = jnp.where(found > 0, start + (before >> 1) + (before & 1) * MAX_PAIRS, -1)
    row = lax.broadcasted_iota(i32, (ROWBLK, slots), 0)
    step = (row >> 2) ^ y
    first = jnp.where(c == 0, 1, 3)
    rel = jnp.where(step == 0, 0, jnp.where(step == first, 1, jnp.where(step == 2, 3, 2)))
    grad = rel * SHARE_BLOCKS + (row & 3)
    code = row * SLOTS + found - 1 + (grad << 9) - NO_BLOCK

    key_t, code_t, start_t = key.T, code.T, start.T
    end_t = start_t + jnp.broadcast_to(pairs, (16, slots)).T
    position = lax.broadcasted_iota(i32, (CALL_SLOTS, 2 * MAX_PAIRS), 1)
    pair = position[:, :MAX_PAIRS]
    for call in range(CALLS):
        rows = slice(call * CALL_SLOTS, (call + 1) * CALL_SLOTS)
        flat = jnp.zeros((CALL_SLOTS, 2 * MAX_PAIRS), i32)
        for r in range(ROWBLK):
            flat = flat + jnp.where(key_t[rows, r : r + 1] == position, code_t[rows, r : r + 1], 0)
        words = jnp.sum(flat, axis=0, keepdims=True) + NO_BLOCK
        ended = jnp.sum(jnp.where(end_t[rows, :1] <= pair, 1, 0), axis=0, keepdims=True)
        opens = jnp.sum(jnp.where(start_t[rows, :1] == pair, 1, 0), axis=0, keepdims=True)
        meta = (jnp.minimum(ended, CALL_SLOTS - 1) + opens * CALL_SLOTS) << 14
        last = end_t[call * CALL_SLOTS + CALL_SLOTS - 1 : (call + 1) * CALL_SLOTS, :1]
        words_refs[call][:, :MAX_PAIRS] = words[:, :MAX_PAIRS] + meta
        words_refs[call][:, MAX_PAIRS : 2 * MAX_PAIRS] = words[:, MAX_PAIRS:]
        words_refs[call][:, 2 * MAX_PAIRS :] = jnp.broadcast_to(last, (1, BLOCK))

def prepare(adj_values, adj_cols, adj_counts, where, gates):
    shape = (ROWBLK * SLOTS, BLOCK, BLOCK)
    words = pltpu.VMEM((1, 2 * MAX_PAIRS + BLOCK), jnp.int32)
    return pl.pallas_call(
        prepare_kernel,
        out_shape=(pltpu.VMEM(shape, jnp.bfloat16),) + (words,) * CALLS,
        in_specs=[IN_SMEM, IN_SMEM, IN_VMEM, ANYWHERE] + [ANYWHERE] * len(gates),
        out_specs=(IN_VMEM,) * (1 + CALLS),
        scratch_shapes=[pltpu.SemaphoreType.DMA],
        compiler_params=pltpu.CompilerParams(vmem_limit_bytes=4 << 20),
        cost_estimate=TINY,
        name="prepare",
    )(
        where,
        pltpu.with_memory_space_constraint(adj_counts.reshape(-1), pltpu.HBM),
        pltpu.with_memory_space_constraint(adj_cols, pltpu.HBM),
        pltpu.with_memory_space_constraint(adj_values.reshape(shape), pltpu.HBM),
        *gates,
    )


TINY = pl.CostEstimate(flops=0, bytes_accessed=1024, transcendentals=0)
ANYWHERE = pl.BlockSpec(memory_space=pl.ANY)
IN_VMEM = pl.BlockSpec(memory_space=pltpu.VMEM)
IN_SMEM = pl.BlockSpec(memory_space=pltpu.SMEM)


def in_vmem(value):
    return pltpu.with_memory_space_constraint(value, pltpu.VMEM)


def load_kernel(grad_ref, preact_ref, feat_ref, own_ref, feat0_ref, feat1_ref, grad, preact, sems):
    first = pltpu.make_async_copy(grad_ref, grad, sems.at[0])
    second = pltpu.make_async_copy(preact_ref, preact, sems.at[1])
    third = pltpu.make_async_copy(feat_ref.at[pl.ds(0, 2)], feat0_ref, sems.at[2])
    fourth = pltpu.make_async_copy(feat_ref.at[pl.ds(2, 2)], feat1_ref, sems.at[3])
    copies = (first, second, third, fourth)
    for copy in copies:
        copy.start()
    for copy in copies:
        copy.wait()
    for b in range(SHARE_BLOCKS):
        value = grad[b].astype(jnp.float32)
        own_ref[b] = jnp.where(preact[b].astype(jnp.float32) > 0, value, 0.0).astype(jnp.bfloat16)


def load(grad_out, preact, features):
    whole, part = (SHARE_BLOCKS, BLOCK, FEAT), (2, BLOCK, FEAT)
    return pl.pallas_call(
        load_kernel,
        out_shape=tuple(pltpu.VMEM(s, jnp.bfloat16) for s in (whole, part, part)),
        in_specs=[ANYWHERE] * 3,
        out_specs=(IN_VMEM,) * 3,
        scratch_shapes=[pltpu.VMEM(whole, jnp.bfloat16)] * 2 + [pltpu.SemaphoreType.DMA((4,))],
        compiler_params=pltpu.CompilerParams(vmem_limit_bytes=4 << 20),
        cost_estimate=TINY,
        name="load",
    )(*(pltpu.with_memory_space_constraint(v.reshape(whole), pltpu.HBM) for v in (grad_out, preact, features)))


def join_kernel(n, *refs):
    out_ref = refs[-1]
    at = 0
    for ref in refs[:n]:
        size = ref.shape[0]
        out_ref[at : at + size] = ref[...]
        at += size
    if at < out_ref.shape[0]:
        out_ref[at:] = jnp.zeros_like(out_ref[at:])


def join(pieces, gates=(), zeros=0):
    size = sum(p.shape[0] for p in pieces) + zeros
    return pl.pallas_call(
        functools.partial(join_kernel, len(pieces)),
        out_shape=pltpu.VMEM((size, *pieces[0].shape[1:]), pieces[0].dtype),
        in_specs=[IN_VMEM] * len(pieces) + [ANYWHERE] * len(gates),
        out_specs=IN_VMEM,
        compiler_params=pltpu.CompilerParams(vmem_limit_bytes=4 << 20),
        cost_estimate=TINY,
        name="join",
    )(*(in_vmem(p) for p in pieces), *gates)


def fold_kernel(n, kept_ref, got_ref, *refs):
    at = 0
    for ref in refs[-n:]:
        size = ref.shape[0]
        for b in range(size):
            ref[b] = (kept_ref[at + b].astype(jnp.float32) + got_ref[at + b].astype(jnp.float32)).astype(jnp.bfloat16)
        at += size


def fold(kept, got, halves, gates=()):
    size, *rest = kept.shape
    out = tuple(pltpu.VMEM((size // halves, *rest), jnp.bfloat16) for _ in range(halves))
    return pl.pallas_call(
        functools.partial(fold_kernel, halves),
        out_shape=out,
        in_specs=[IN_VMEM] * 2 + [ANYWHERE] * len(gates),
        out_specs=(IN_VMEM,) * halves,
        compiler_params=pltpu.CompilerParams(vmem_limit_bytes=4 << 20),
        cost_estimate=TINY,
        name="fold",
    )(in_vmem(kept), in_vmem(got), *gates)


def ring_kernel(own_ref, opposite_ref, left_ref, right_ref, *refs):
    own, opposite, left, right = (
        r[...].astype(jnp.float32) for r in (own_ref, opposite_ref, left_ref, right_ref)
    )
    refs[-1][...] = ((own + opposite) + (left + right)).astype(jnp.bfloat16)


def ring_sum(own, got, gates=()):
    return pl.pallas_call(
        ring_kernel,
        out_shape=pltpu.VMEM(own.shape, jnp.bfloat16),
        in_specs=[IN_VMEM] * 4 + [ANYWHERE] * len(gates),
        out_specs=IN_VMEM,
        compiler_params=pltpu.CompilerParams(vmem_limit_bytes=4 << 20),
        cost_estimate=TINY,
        name="ring_sum",
    )(in_vmem(own), *(in_vmem(v) for v in got), *gates)


def features_kernel(first_ref, second_ref, weight_ref, out_ref):
    for k, ref in enumerate((first_ref, second_ref)):
        for b in range(2):
            rows = pl.ds((2 * k + b) * BLOCK, BLOCK)
            value = lax.dot_general(
                ref[b], weight_ref[...], (((1,), (1,)), ((), ())), preferred_element_type=jnp.float32
            )
            out_ref[rows, :] = value.astype(jnp.bfloat16)


def features_gradient(first, second, weight):
    return pl.pallas_call(
        features_kernel,
        out_shape=jax.ShapeDtypeStruct((SHARE_BLOCKS * BLOCK, FEAT), jnp.bfloat16),
        in_specs=[IN_VMEM] * 3,
        out_specs=IN_VMEM,
        compiler_params=pltpu.CompilerParams(vmem_limit_bytes=4 << 20),
        cost_estimate=TINY,
        name="features_gradient",
    )(in_vmem(first), in_vmem(second), weight)


def weight_kernel(core_ref, *refs):
    ins, outs = refs[:-2], refs[-2:]
    n = FEAT // 2
    for k, out_ref in enumerate(outs):
        rows = pl.ds(pl.multiple_of((core_ref[0] ^ k) * n, n), n)
        total = jnp.zeros((n, FEAT), jnp.float32)
        for feat, held in zip(ins[::2], ins[1::2]):
            size = feat.shape[0] * BLOCK
            left = feat[:, :, rows].reshape(size, n)
            total = total + lax.dot_general(
                left, held[...].reshape(size, FEAT), (((0,), (0,)), ((), ())), preferred_element_type=jnp.float32
            )
        out_ref[...] = total.astype(out_ref.dtype)


def weight_terms(core, pairs):
    flat = [in_vmem(v) for pair in pairs for v in pair]
    return pl.pallas_call(
        weight_kernel,
        out_shape=tuple(pltpu.VMEM((FEAT // 2, FEAT), t) for t in (jnp.float32, jnp.bfloat16)),
        in_specs=[IN_SMEM] + [IN_VMEM] * len(flat),
        out_specs=(IN_VMEM,) * 2,
        compiler_params=pltpu.CompilerParams(vmem_limit_bytes=8 << 20),
        cost_estimate=TINY,
        name="weight_terms",
    )(core.reshape(1), *flat)


def products_kernel(words_ref, grad_ref, adj_ref, *refs):
    out_ref = refs[-1]

    def pair(p, acc):
        w0 = words_ref[0, p]
        w1 = words_ref[0, MAX_PAIRS + p]
        slot = (w0 >> 14) & (CALL_SLOTS - 1)
        keep = jnp.where((w0 >> 19) == 0, 1.0, 0.0).astype(jnp.float32)
        grad = jnp.concatenate([grad_ref[(w0 >> 9) & 31], grad_ref[(w1 >> 9) & 31]], axis=0)
        adj = jnp.concatenate([adj_ref[w0 & 511], adj_ref[w1 & 511]], axis=0)
        term = lax.dot_general(adj, grad, (((0,), (0,)), ((), ())), preferred_element_type=jnp.float32)
        acc = acc * keep + term
        out_ref[slot] = acc.astype(jnp.bfloat16)
        return acc

    def steps(i, acc):
        for u in range(UNROLL):
            acc = pair(i * UNROLL + u, acc)
        return acc

    count = (words_ref[0, 2 * MAX_PAIRS] + UNROLL - 1) // UNROLL
    lax.fori_loop(0, count, steps, jnp.zeros((BLOCK, FEAT), jnp.float32))


def products(name, words, grad, adj, gates):
    return pl.pallas_call(
        products_kernel,
        out_shape=pltpu.VMEM((CALL_SLOTS, BLOCK, FEAT), jnp.bfloat16),
        in_specs=[IN_SMEM, IN_VMEM, IN_VMEM] + [ANYWHERE] * len(gates),
        out_specs=IN_VMEM,
        compiler_params=pltpu.CompilerParams(vmem_limit_bytes=4 << 20),
        cost_estimate=TINY,
        name=f"products_{name}",
    )(
        words,
        in_vmem(grad),
        in_vmem(adj),
        *gates,
    )


def body(grad_out, preact, features, weight, adj_values, adj_cols, adj_counts):
    row, y = lax.axis_index("row"), lax.axis_index("rep")
    z, x, c = row // (2 * RING), row // 2 % RING, row % 2
    core = c.astype(jnp.int32)

    own, *mine = load(grad_out, preact, features)
    got = exchange(own, "y0", "y1")
    near = [exchange(mine[p], ORDER[p][0][3], ORDER[p][1][3]) for p in (0, 1)]
    half = join([own, got], near)
    got = exchange(half, "y1", "y0")
    feats = [join([mine[p], near[p]], [half]) for p in (0, 1)]
    far = [exchange(feats[p], ORDER[p][0][2], ORDER[p][1][2]) for p in (0, 1)]
    where = jnp.stack([z, x, c, y]).astype(jnp.int32)
    adj, *words = prepare(adj_values, adj_cols, adj_counts, where, feats)
    grad = join([half, got], [adj, *far], zeros=1)

    def product(sent, upper, gates=()):
        call = sent * 2 + upper
        return products(call, words[call], grad, adj, gates)

    sent_upper = product(1, 1)
    sent_lower = product(1, 0, [sent_upper])
    kept_upper = product(0, 1, [sent_lower])
    upper = list(fold(kept_upper, swap_cores(sent_upper), 2))
    kept_lower = product(0, 0, upper)
    lower = list(fold(kept_lower, swap_cores(sent_lower), 2))

    def halve(step, gates=()):
        for p in (0, 1):
            got = exchange(upper[p], ORDER[p][0][step], ORDER[p][1][step])
            lower[p], *rest = fold(lower[p], got, 2 if step < 3 else 1, gates)
            upper[p] = rest[0] if rest else None
        return list(lower)

    halve(0)
    halve(1)
    held = [(v[p], w[p]) for p in (0, 1) for v, w in ((feats, lower), (far, upper))]
    term, other = weight_terms(core, held)
    (term,) = fold(term, swap_cores(other), 1)
    upper[1] = join([upper[1]], [term])
    for k, rings in enumerate((("x", "z"), ("z", "x"), ("y", "y"))):
        got = [shift(term, *rings, hops) for hops in (2, 1, 3)]
        term = ring_sum(term, got, lower)
        if k < 2:
            halve(2 + k, [term])
    theirs = swap_cores(term)
    grad_weight = jnp.concatenate([jnp.where(c == 0, term, theirs), jnp.where(c == 0, theirs, term)])
    return features_gradient(*lower, weight), grad_weight.astype(jnp.float32)


def solution(mesh):
    placed = (
        P(AXES, None),
        P(AXES, None),
        P(AXES, None),
        P(),
        P("row", "rep", None, None),
        P("row", "rep"),
        P("row", "rep"),
    )
    return jax.shard_map(body, mesh=mesh, in_specs=placed, out_specs=(P(AXES, None), P()), check_vma=False)
```

```python
import functools

import jax
import jax.numpy as jnp
from jax import lax
from jax.experimental import pallas as pl
from jax.experimental.pallas import tpu as pltpu
from jax.sharding import PartitionSpec as P

AXES = ("row", "rep")
RING = 4
BLOCK = 128
FEAT = 256
SHARE_BLOCKS = 4
ROWBLK = 16
SLOTS = 32
CALLS = 4
CALL_SLOTS = 32
MAX_PAIRS = 256
UNROLL = 16
NO_BLOCK = ROWBLK << 9

FLIP = {"x0": ("x", 1), "x1": ("x", 3), "z0": ("z", 1), "z1": ("z", 3), "y0": ("y", 1), "y1": ("y", 3)}
ORDER = (
    (("x0", "z0", "x1", "z1"), ("z0", "x0", "z1", "x1")),
    (("x1", "z1", "x0", "z0"), ("z1", "x1", "z0", "x0")),
)


def linear(z, x, c, y):
    return ((z * RING + x) * 2 + c) * RING + y


def exchange_pairs(first, second):
    pairs = []
    for z in range(RING):
        for x in range(RING):
            for c in range(2):
                for y in range(RING):
                    at = {"z": z, "x": x, "c": c, "y": y}
                    axis, mask = FLIP[first if c == 0 else second]
                    at[axis] ^= mask
                    pairs.append((linear(z, x, c, y), linear(**at)))
    return pairs


def exchange(value, first, second):
    return lax.ppermute(value, AXES, exchange_pairs(first, second))


def shift(value, first, second, hops):
    pairs = []
    for z in range(RING):
        for x in range(RING):
            for c in range(2):
                for y in range(RING):
                    at = {"z": z, "x": x, "c": c, "y": y}
                    axis = first if c == 0 else second
                    at[axis] = (at[axis] + hops) % RING
                    pairs.append((linear(z, x, c, y), linear(**at)))
    return lax.ppermute(value, AXES, pairs)


def swap_cores(value):
    pairs = [(d, d ^ RING) for d in range(RING * RING * 2 * RING)]
    return lax.ppermute(value, AXES, pairs)


def prepare_kernel(where_ref, counts_ref, cols_ref, adj_ref, *refs):
    out_ref, words_refs, sem = refs[-CALLS - 2], refs[-CALLS - 1 : -1], refs[-1]

    def copies(action):
        for r in range(ROWBLK):
            count = counts_ref[r]
            for bit in range(6):
                size = 1 << bit
                offset = r * SLOTS + (count & ~(2 * size - 1))

                @pl.when((count & size) != 0)
                def _(offset=offset, size=size):
                    at = pl.ds(offset, size)
                    action(pltpu.make_async_copy(adj_ref.at[at], out_ref.at[at], sem))

    copies(lambda copy: copy.start())
    plan(where_ref, counts_ref, cols_ref, words_refs)
    copies(lambda copy: copy.wait())


def plan(where_ref, counts_ref, cols_ref, words_refs):
    i32 = jnp.int32
    z, x, c, y = (where_ref[i] for i in range(4))
    slots = CALLS * CALL_SLOTS

    lane = lax.broadcasted_iota(i32, (8, slots), 1)
    sent, upper, part = lane >> 6, (lane >> 5) & 1, (lane >> 4) & 1
    core = c ^ sent
    place = upper * 8 + ((lane & 15) >> 1)
    at = {"z": jnp.zeros_like(lane) + z, "x": jnp.zeros_like(lane) + x}
    for bit in range(4):
        on = (place >> (3 - bit)) & 1
        for p in range(2):
            for k in range(2):
                axis, mask = FLIP[ORDER[p][k][bit]]
                at[axis] = at[axis] ^ jnp.where((part == p) & (core == k), on * mask, 0)
    group = (at["z"] * RING + at["x"]) * 2 + core
    target = (group * ROWBLK + y * SHARE_BLOCKS + part * 2 + (lane & 1))[:1]

    index = lax.broadcasted_iota(i32, (ROWBLK, SLOTS), 0)
    live = jnp.zeros((ROWBLK, SLOTS), i32)
    for r in range(ROWBLK):
        live = jnp.where(index == r, counts_ref[r], live)
    cols = jnp.where(lax.broadcasted_iota(i32, (ROWBLK, SLOTS), 1) < live, cols_ref[...], -1)
    found = jnp.zeros((ROWBLK, slots), i32)
    for s in range(SLOTS):
        found = found + jnp.where(cols[:, s : s + 1] == target, s + 1, 0)
    present = jnp.where(found > 0, 1, 0)
    before, count = [], jnp.zeros((1, slots), i32)
    for r in range(ROWBLK):
        before.append(count)
        count = count + present[r : r + 1]
    before = jnp.concatenate(before, axis=0)
    pairs = jnp.maximum((count + 1) >> 1, 1)
    i0 = lax.broadcasted_iota(i32, (slots, slots), 0)
    i1 = lax.broadcasted_iota(i32, (slots, slots), 1)
    earlier = jnp.where((i0 >> 5 == i1 >> 5) & (i0 < i1), 1.0, 0.0).astype(jnp.bfloat16)
    wide = jnp.broadcast_to(pairs, (16, slots)).astype(jnp.float32).astype(jnp.bfloat16)
    start = jnp.dot(wide, earlier, preferred_element_type=jnp.float32).astype(i32)

    key = jnp.where(found > 0, start + (before >> 1) + (before & 1) * MAX_PAIRS, -1)
    row = lax.broadcasted_iota(i32, (ROWBLK, slots), 0)
    step = (row >> 2) ^ y
    first = jnp.where(c == 0, 1, 3)
    rel = jnp.where(step == 0, 0, jnp.where(step == first, 1, jnp.where(step == 2, 3, 2)))
    grad = rel * SHARE_BLOCKS + (row & 3)
    code = row * SLOTS + found - 1 + (grad << 9) - NO_BLOCK

    key_t, code_t, start_t = key.T, code.T, start.T
    end_t = start_t + jnp.broadcast_to(pairs, (16, slots)).T
    position = lax.broadcasted_iota(i32, (CALL_SLOTS, 2 * MAX_PAIRS), 1)
    pair = position[:, :MAX_PAIRS]
    for call in range(CALLS):
        rows = slice(call * CALL_SLOTS, (call + 1) * CALL_SLOTS)
        flat = jnp.zeros((CALL_SLOTS, 2 * MAX_PAIRS), i32)
        for r in range(ROWBLK):
            flat = flat + jnp.where(key_t[rows, r : r + 1] == position, code_t[rows, r : r + 1], 0)
        words = jnp.sum(flat, axis=0, keepdims=True) + NO_BLOCK
        ended = jnp.sum(jnp.where(end_t[rows, :1] <= pair, 1, 0), axis=0, keepdims=True)
        opens = jnp.sum(jnp.where(start_t[rows, :1] == pair, 1, 0), axis=0, keepdims=True)
        meta = (jnp.minimum(ended, CALL_SLOTS - 1) + opens * CALL_SLOTS) << 14
        last = end_t[call * CALL_SLOTS + CALL_SLOTS - 1 : (call + 1) * CALL_SLOTS, :1]
        words_refs[call][:, :MAX_PAIRS] = words[:, :MAX_PAIRS] + meta
        words_refs[call][:, MAX_PAIRS : 2 * MAX_PAIRS] = words[:, MAX_PAIRS:]
        words_refs[call][:, 2 * MAX_PAIRS :] = jnp.broadcast_to(last, (1, BLOCK))

def prepare(adj_values, adj_cols, adj_counts, where, gates):
    shape = (ROWBLK * SLOTS, BLOCK, BLOCK)
    words = pltpu.VMEM((1, 2 * MAX_PAIRS + BLOCK), jnp.int32)
    return pl.pallas_call(
        prepare_kernel,
        out_shape=(pltpu.VMEM(shape, jnp.bfloat16),) + (words,) * CALLS,
        in_specs=[IN_SMEM, IN_SMEM, IN_VMEM, ANYWHERE] + [ANYWHERE] * len(gates),
        out_specs=(IN_VMEM,) * (1 + CALLS),
        scratch_shapes=[pltpu.SemaphoreType.DMA],
        compiler_params=pltpu.CompilerParams(vmem_limit_bytes=4 << 20),
        cost_estimate=TINY,
        name="prepare",
    )(
        where,
        pltpu.with_memory_space_constraint(adj_counts.reshape(-1), pltpu.HBM),
        pltpu.with_memory_space_constraint(adj_cols, pltpu.HBM),
        pltpu.with_memory_space_constraint(adj_values.reshape(shape), pltpu.HBM),
        *gates,
    )


TINY = pl.CostEstimate(flops=0, bytes_accessed=1024, transcendentals=0)
ANYWHERE = pl.BlockSpec(memory_space=pl.ANY)
IN_VMEM = pl.BlockSpec(memory_space=pltpu.VMEM)
IN_SMEM = pl.BlockSpec(memory_space=pltpu.SMEM)


def in_vmem(value):
    return pltpu.with_memory_space_constraint(value, pltpu.VMEM)


def load_kernel(grad_ref, preact_ref, feat_ref, own_ref, feat0_ref, feat1_ref, grad, preact, sems):
    first = pltpu.make_async_copy(grad_ref, grad, sems.at[0])
    second = pltpu.make_async_copy(preact_ref, preact, sems.at[1])
    third = pltpu.make_async_copy(feat_ref.at[pl.ds(0, 2)], feat0_ref, sems.at[2])
    fourth = pltpu.make_async_copy(feat_ref.at[pl.ds(2, 2)], feat1_ref, sems.at[3])
    copies = (first, second, third, fourth)
    for copy in copies:
        copy.start()
    for copy in copies:
        copy.wait()
    for b in range(SHARE_BLOCKS):
        value = grad[b].astype(jnp.float32)
        own_ref[b] = jnp.where(preact[b].astype(jnp.float32) > 0, value, 0.0).astype(jnp.bfloat16)


def load(grad_out, preact, features):
    whole, part = (SHARE_BLOCKS, BLOCK, FEAT), (2, BLOCK, FEAT)
    return pl.pallas_call(
        load_kernel,
        out_shape=tuple(pltpu.VMEM(s, jnp.bfloat16) for s in (whole, part, part)),
        in_specs=[ANYWHERE] * 3,
        out_specs=(IN_VMEM,) * 3,
        scratch_shapes=[pltpu.VMEM(whole, jnp.bfloat16)] * 2 + [pltpu.SemaphoreType.DMA((4,))],
        compiler_params=pltpu.CompilerParams(vmem_limit_bytes=4 << 20),
        cost_estimate=TINY,
        name="load",
    )(*(pltpu.with_memory_space_constraint(v.reshape(whole), pltpu.HBM) for v in (grad_out, preact, features)))


def join_kernel(n, *refs):
    out_ref = refs[-1]
    at = 0
    for ref in refs[:n]:
        size = ref.shape[0]
        out_ref[at : at + size] = ref[...]
        at += size
    if at < out_ref.shape[0]:
        out_ref[at:] = jnp.zeros_like(out_ref[at:])


def join(pieces, gates=(), zeros=0):
    size = sum(p.shape[0] for p in pieces) + zeros
    return pl.pallas_call(
        functools.partial(join_kernel, len(pieces)),
        out_shape=pltpu.VMEM((size, *pieces[0].shape[1:]), pieces[0].dtype),
        in_specs=[IN_VMEM] * len(pieces) + [ANYWHERE] * len(gates),
        out_specs=IN_VMEM,
        compiler_params=pltpu.CompilerParams(vmem_limit_bytes=4 << 20),
        cost_estimate=TINY,
        name="join",
    )(*(in_vmem(p) for p in pieces), *gates)


def fold_kernel(n, kept_ref, got_ref, *refs):
    at = 0
    for ref in refs[-n:]:
        size = ref.shape[0]
        for b in range(size):
            ref[b] = (kept_ref[at + b].astype(jnp.float32) + got_ref[at + b].astype(jnp.float32)).astype(jnp.bfloat16)
        at += size


def fold(kept, got, halves, gates=()):
    size, *rest = kept.shape
    out = tuple(pltpu.VMEM((size // halves, *rest), jnp.bfloat16) for _ in range(halves))
    return pl.pallas_call(
        functools.partial(fold_kernel, halves),
        out_shape=out,
        in_specs=[IN_VMEM] * 2 + [ANYWHERE] * len(gates),
        out_specs=(IN_VMEM,) * halves,
        compiler_params=pltpu.CompilerParams(vmem_limit_bytes=4 << 20),
        cost_estimate=TINY,
        name="fold",
    )(in_vmem(kept), in_vmem(got), *gates)


def fold_through_kernel(kept_ref, got_ref, value_ref, out_ref, through_ref):
    out_ref[...] = (kept_ref[...].astype(jnp.float32) + got_ref[...].astype(jnp.float32)).astype(jnp.bfloat16)
    through_ref[...] = value_ref[...]


def fold_through(kept, got, value):
    return pl.pallas_call(
        fold_through_kernel,
        out_shape=tuple(pltpu.VMEM(v.shape, jnp.bfloat16) for v in (kept, value)),
        in_specs=[IN_VMEM] * 3,
        out_specs=(IN_VMEM,) * 2,
        compiler_params=pltpu.CompilerParams(vmem_limit_bytes=4 << 20),
        cost_estimate=TINY,
        name="fold_through",
    )(*(in_vmem(v) for v in (kept, got, value)))


def join_two_kernel(*refs):
    for p, out_ref in enumerate(refs[-2:]):
        size = refs[p].shape[0]
        out_ref[:size] = refs[p][...]
        out_ref[size:] = refs[2 + p][...]


def join_two(first, second, gate):
    out = tuple(pltpu.VMEM((2 * v.shape[0], *v.shape[1:]), v.dtype) for v in first)
    return pl.pallas_call(
        join_two_kernel,
        out_shape=out,
        in_specs=[IN_VMEM] * 4 + [ANYWHERE],
        out_specs=(IN_VMEM,) * 2,
        compiler_params=pltpu.CompilerParams(vmem_limit_bytes=4 << 20),
        cost_estimate=TINY,
        name="join_two",
    )(*(in_vmem(v) for v in (*first, *second)), gate)


def ring_kernel(own_ref, opposite_ref, left_ref, right_ref, *refs):
    own, opposite, left, right = (
        r[...].astype(jnp.float32) for r in (own_ref, opposite_ref, left_ref, right_ref)
    )
    refs[-1][...] = ((own + opposite) + (left + right)).astype(jnp.bfloat16)


def ring_sum(own, got, gates=()):
    return pl.pallas_call(
        ring_kernel,
        out_shape=pltpu.VMEM(own.shape, jnp.bfloat16),
        in_specs=[IN_VMEM] * 4 + [ANYWHERE] * len(gates),
        out_specs=IN_VMEM,
        compiler_params=pltpu.CompilerParams(vmem_limit_bytes=4 << 20),
        cost_estimate=TINY,
        name="ring_sum",
    )(in_vmem(own), *(in_vmem(v) for v in got), *gates)


def features_kernel(first_ref, second_ref, weight_ref, out_ref):
    for k, ref in enumerate((first_ref, second_ref)):
        for b in range(2):
            rows = pl.ds((2 * k + b) * BLOCK, BLOCK)
            value = lax.dot_general(
                ref[b], weight_ref[...], (((1,), (1,)), ((), ())), preferred_element_type=jnp.float32
            )
            out_ref[rows, :] = value.astype(jnp.bfloat16)


def features_gradient(first, second, weight):
    return pl.pallas_call(
        features_kernel,
        out_shape=jax.ShapeDtypeStruct((SHARE_BLOCKS * BLOCK, FEAT), jnp.bfloat16),
        in_specs=[IN_VMEM] * 3,
        out_specs=IN_VMEM,
        compiler_params=pltpu.CompilerParams(vmem_limit_bytes=4 << 20),
        cost_estimate=TINY,
        name="features_gradient",
    )(in_vmem(first), in_vmem(second), weight)


def weight_kernel(core_ref, *refs):
    ins, outs = refs[:-2], refs[-2:]
    n = FEAT // 2
    for k, out_ref in enumerate(outs):
        rows = pl.ds(pl.multiple_of((core_ref[0] ^ k) * n, n), n)
        total = jnp.zeros((n, FEAT), jnp.float32)
        for feat, held in zip(ins[::2], ins[1::2]):
            size = feat.shape[0] * BLOCK
            left = feat[:, :, rows].reshape(size, n)
            total = total + lax.dot_general(
                left, held[...].reshape(size, FEAT), (((0,), (0,)), ((), ())), preferred_element_type=jnp.float32
            )
        out_ref[...] = total.astype(out_ref.dtype)


def weight_terms(core, pairs):
    flat = [in_vmem(v) for pair in pairs for v in pair]
    return pl.pallas_call(
        weight_kernel,
        out_shape=tuple(pltpu.VMEM((FEAT // 2, FEAT), t) for t in (jnp.float32, jnp.bfloat16)),
        in_specs=[IN_SMEM] + [IN_VMEM] * len(flat),
        out_specs=(IN_VMEM,) * 2,
        compiler_params=pltpu.CompilerParams(vmem_limit_bytes=8 << 20),
        cost_estimate=TINY,
        name="weight_terms",
    )(core.reshape(1), *flat)


def products_kernel(words_ref, grad_ref, adj_ref, *refs):
    out_ref = refs[-1]

    def pair(p, acc):
        w0 = words_ref[0, p]
        w1 = words_ref[0, MAX_PAIRS + p]
        slot = (w0 >> 14) & (CALL_SLOTS - 1)
        keep = jnp.where((w0 >> 19) == 0, 1.0, 0.0).astype(jnp.float32)
        grad = jnp.concatenate([grad_ref[(w0 >> 9) & 31], grad_ref[(w1 >> 9) & 31]], axis=0)
        adj = jnp.concatenate([adj_ref[w0 & 511], adj_ref[w1 & 511]], axis=0)
        term = lax.dot_general(adj, grad, (((0,), (0,)), ((), ())), preferred_element_type=jnp.float32)
        acc = acc * keep + term
        out_ref[slot] = acc.astype(jnp.bfloat16)
        return acc

    def steps(i, acc):
        for u in range(UNROLL):
            acc = pair(i * UNROLL + u, acc)
        return acc

    count = (words_ref[0, 2 * MAX_PAIRS] + UNROLL - 1) // UNROLL
    lax.fori_loop(0, count, steps, jnp.zeros((BLOCK, FEAT), jnp.float32))


def products(name, words, grad, adj, gates):
    return pl.pallas_call(
        products_kernel,
        out_shape=pltpu.VMEM((CALL_SLOTS, BLOCK, FEAT), jnp.bfloat16),
        in_specs=[IN_SMEM, IN_VMEM, IN_VMEM] + [ANYWHERE] * len(gates),
        out_specs=IN_VMEM,
        compiler_params=pltpu.CompilerParams(vmem_limit_bytes=4 << 20),
        cost_estimate=TINY,
        name=f"products_{name}",
    )(
        words,
        in_vmem(grad),
        in_vmem(adj),
        *gates,
    )


def body(grad_out, preact, features, weight, adj_values, adj_cols, adj_counts):
    row, y = lax.axis_index("row"), lax.axis_index("rep")
    z, x, c = row // (2 * RING), row // 2 % RING, row % 2
    core = c.astype(jnp.int32)

    own, *mine = load(grad_out, preact, features)
    got = exchange(own, "y0", "y1")
    near = [exchange(mine[p], ORDER[p][0][3], ORDER[p][1][3]) for p in (0, 1)]
    half = join([own, got], near)
    got = exchange(half, "y1", "y0")
    feats = join_two(mine, near, half)
    far = [exchange(feats[p], ORDER[p][0][2], ORDER[p][1][2]) for p in (0, 1)]
    where = jnp.stack([z, x, c, y]).astype(jnp.int32)
    adj, *words = prepare(adj_values, adj_cols, adj_counts, where, feats)
    grad = join([half, got], [adj, *far], zeros=1)

    def product(sent, upper, gates=()):
        call = sent * 2 + upper
        return products(call, words[call], grad, adj, gates)

    sent_upper = product(1, 1)
    sent_lower = product(1, 0, [sent_upper])
    kept_upper = product(0, 1, [sent_lower])
    upper = list(fold(kept_upper, swap_cores(sent_upper), 2))
    kept_lower = product(0, 0, upper)
    lower = list(fold(kept_lower, swap_cores(sent_lower), 2))

    def halve(step, gates=()):
        for p in (0, 1):
            got = exchange(upper[p], ORDER[p][0][step], ORDER[p][1][step])
            lower[p], *rest = fold(lower[p], got, 2 if step < 3 else 1, gates)
            upper[p] = rest[0] if rest else None
        return list(lower)

    halve(0)
    halve(1)
    held = [(v[p], w[p]) for p in (0, 1) for v, w in ((feats, lower), (far, upper))]
    term, other = weight_terms(core, held)
    term, upper[1] = fold_through(term, swap_cores(other), upper[1])
    for k, rings in enumerate((("x", "z"), ("z", "x"), ("y", "y"))):
        got = [shift(term, *rings, hops) for hops in (2, 1, 3)]
        term = ring_sum(term, got, lower)
        if k < 2:
            halve(2 + k, [term])
    theirs = swap_cores(term)
    grad_weight = jnp.concatenate([jnp.where(c == 0, term, theirs), jnp.where(c == 0, theirs, term)])
    return features_gradient(*lower, weight), grad_weight.astype(jnp.float32)


def solution(mesh):
    placed = (
        P(AXES, None),
        P(AXES, None),
        P(AXES, None),
        P(),
        P("row", "rep", None, None),
        P("row", "rep"),
        P("row", "rep"),
    )
    return jax.shard_map(body, mesh=mesh, in_specs=placed, out_specs=(P(AXES, None), P()), check_vma=False)
```
